128 devices in a mesh: shard: 64 (over z, y, x), grp: 2 (over core).
Axes of the slice: x: 4, y: 4, z: 4, core: 2. Of those that a mesh axis runs over, the one named last changes fastest.
Arguments:
- embeddings: bfloat16 [262144, 1024], P(('shard', 'grp'))
- send_row: int32 [128, 2048], P(('shard', 'grp')), may hold values from -1 to 2047, as said below
- slot_cluster: int32 [262144], P('shard'), may hold values from -1 to 15, as said below
Outputs:
- dup_score: float32 [262144], P(('shard', 'grp'))
The draws below stay inside these ranges and needn't reach their ends.
Inputs may be any that keep to these rules, and one draw needn't show every extreme that they name: `send_row`: in each device's row, a local row index appears at most once; for destination d the used entries are the first ones, slots d * 16 to d * 16 + n - 1 with n from 1 to 16; some destination receives 16 rows from every device. slot_cluster[d * 2048 + s * 16 + k] is -1 exactly where send_row[s, d * 16 + k] is -1.
All inputs are finite; a program needn't handle non-finite values.
Results may differ from the reference program's by a relative error of at most 0.00031.
Values may be sent and summed in bfloat16 or wider, within the bound.
No kernel may reach another device: no remote copies, remote signals or barrier semaphores. Data moves between devices by JAX's collectives and lax.ppermute only.
A program may use at most 64 MiB of HBM per device.

```python
import jax
import jax.numpy as jnp
from jax import lax

D = 1024
ROWS_DEV = 2048
KCL = 16
CAP = 16
N_SHARD = 64
N_GRP = 2
DEVICES = 128


def layout(key):
    total = DEVICES
    keys = jax.random.split(key, 4)
    counts = jax.random.randint(keys[0], (total, total), 1, CAP + 1)
    offsets = jax.random.randint(keys[1], (2,), 0, total)
    ranks = jnp.arange(total, dtype=jnp.int32)
    column = ranks[None, :]
    counts = jnp.where(column == (ranks[:, None] + offsets[0] + 1) % total, 1, counts)
    counts = jnp.where(column == (ranks[:, None] + offsets[0]) % total, CAP, counts)
    counts = jnp.where(column == offsets[1], CAP, counts)
    slots = jnp.arange(CAP, dtype=jnp.int32)
    valid = slots[None, None, :] < counts[:, :, None]
    flat = valid.reshape(total, total * CAP).astype(jnp.int32)
    rank = jnp.cumsum(flat, axis=1) - 1
    perm_keys = jax.random.split(keys[2], total)
    perms = jax.vmap(lambda k: jax.random.permutation(k, ROWS_DEV))(perm_keys).astype(jnp.int32)
    positions = jnp.arange(ROWS_DEV, dtype=jnp.int32)[None, :]
    perms = jnp.where(perms == ROWS_DEV - 1, perms[:, :1], jnp.where(positions == 0, ROWS_DEV - 1, perms))
    local = jnp.take_along_axis(perms, jnp.maximum(rank, 0), axis=1)
    send_row = jnp.where(flat == 1, local, -1)
    labels = jax.random.randint(keys[3], (total, total, CAP), 0, KCL)
    labels = labels.at[:, 0, 0].set(KCL - 1)
    valid_recv = valid.transpose(1, 0, 2)
    slot_cluster = jnp.where(valid_recv, labels, -1).reshape(-1)
    cid = ranks[:, None, None] // N_GRP * KCL + labels
    cid_send = cid.transpose(1, 0, 2).reshape(total, total * CAP)
    target = jnp.where(flat == 1, ranks[:, None] * ROWS_DEV + local, total * ROWS_DEV)
    row_cluster = jnp.full((total * ROWS_DEV,), -1, jnp.int32).at[target.reshape(-1)].set(cid_send.reshape(-1), mode='drop')
    return (send_row, slot_cluster, row_cluster)


def draw_send_row(key, part):
    return layout(key)[0]


def draw_slot_cluster(key, part):
    return layout(key)[1]


def draw_embeddings(key, part):
    row_cluster = layout(key)[2]
    key = jax.random.fold_in(key, 7)
    keys = jax.random.split(key, 4)
    total_rows = DEVICES * ROWS_DEV
    centers = jax.random.normal(keys[0], (N_SHARD * KCL, D), jnp.float32)
    amplitude = jax.random.uniform(keys[1], (total_rows, 1), jnp.float32, 0.3, 3.0)
    scale = jnp.exp(jax.random.uniform(keys[2], (total_rows, 1), jnp.float32, 0.0, 2.4))
    noise = jax.random.normal(keys[3], (total_rows, D), jnp.float32)
    member = (row_cluster >= 0)[:, None]
    shared = jnp.where(member, centers[jnp.maximum(row_cluster, 0)], 0.0)
    return (scale * (noise + amplitude * shared)).astype(jnp.bfloat16)


def setup_inputs(seed: int = 0) -> dict:
    key_of = jax.random.split(jax.random.key(seed), 4)
    embeddings = draw_embeddings(jax.random.fold_in(key_of[3], 71), 0)
    send_row = draw_send_row(jax.random.fold_in(key_of[3], 71), 0)
    slot_cluster = draw_slot_cluster(jax.random.fold_in(key_of[3], 71), 0)
    return {"embeddings": embeddings, "send_row": send_row, "slot_cluster": slot_cluster}


def reference(embeddings, send_row, slot_cluster):
    lists = send_row.reshape(DEVICES, DEVICES, CAP).transpose(1, 0, 2).reshape(DEVICES, DEVICES * CAP)
    source = jnp.arange(DEVICES * CAP, dtype=jnp.int32) // CAP * ROWS_DEV
    group_rows = N_GRP * ROWS_DEV
    lists_g = lists.reshape(N_SHARD, group_rows)
    source_g = jnp.tile(source, N_GRP)
    labels_g = slot_cluster.reshape(N_SHARD, group_rows)

    def one_group(g):
        lst = lists_g[g]
        valid = lst >= 0
        index = jnp.where(valid, source_g + lst, 0).astype(jnp.int32)
        held = jnp.where(valid[:, None], embeddings[index].astype(jnp.float32), 0.0)
        squares = lax.optimization_barrier(lax.optimization_barrier(jnp.sum(held * held, axis=1, keepdims=True)))
        unit = (held * lax.rsqrt(squares + 1e-06)).astype(jnp.bfloat16)
        labels = labels_g[g]
        ids = jnp.arange(group_rows, dtype=jnp.int32)

        def one_block(b):
            start = (b * ROWS_DEV).astype(jnp.int32)
            left = lax.dynamic_slice_in_dim(unit, start, ROWS_DEV, 0)
            left_lab = lax.dynamic_slice_in_dim(labels, start, ROWS_DEV, 0)
            left_ids = start + jnp.arange(ROWS_DEV, dtype=jnp.int32)
            scores = jnp.dot(left, unit.T, preferred_element_type=jnp.float32)
            keep = (left_lab[:, None] == labels[None, :]) & (left_lab[:, None] >= 0) & (left_ids[:, None] != ids[None, :])
            best = lax.optimization_barrier(jnp.max(jnp.where(keep, scores, jnp.float32(-2.0)), axis=1))
            return jnp.maximum(best, jnp.float32(-1.0))
        return lax.map(one_block, jnp.arange(N_GRP, dtype=jnp.int32))
    out = lax.map(one_group, jnp.arange(N_SHARD, dtype=jnp.int32))
    return out.reshape(-1)
```

```python
import functools

import jax
import jax.numpy as jnp
from jax import lax
from jax.experimental import pallas as pl
from jax.experimental.pallas import tpu as pltpu
from jax.sharding import PartitionSpec as P

LANES = 128
BLOCK = 256
VMEM_LIMIT = 56 << 20
ROWS_BY_ROWS = (((1,), (1,)), ((), ()))


def down_lanes(row):
    parts = [
        jnp.transpose(jnp.broadcast_to(row[:, j : j + LANES], (LANES, LANES)))
        for j in range(0, row.shape[1], LANES)
    ]
    return jnp.concatenate(parts, axis=0)


def fold_lanes(values):
    best = values[:, :LANES]
    for j in range(LANES, values.shape[1], LANES):
        best = jnp.maximum(best, values[:, j : j + LANES])
    return best


def across(values):
    parts = [
        jnp.max(jnp.transpose(values[i : i + LANES]), axis=0, keepdims=True)
        for i in range(0, values.shape[0], LANES)
    ]
    return jnp.concatenate(parts, axis=1)


def same_label(down, labels):
    return jnp.concatenate(
        [down == labels[:, j : j + LANES] for j in range(0, labels.shape[1], LANES)], axis=1
    )


def unit_rows_kernel(index_ref, rows_ref, unit_ref):
    total = rows_ref.shape[0]
    block = total // 2
    lane = lax.broadcasted_iota(jnp.int32, (block, LANES), 1)

    def step(b):
        start = pl.multiple_of(b * block, block)
        index = down_lanes(index_ref[:, pl.ds(start, block)])
        chosen = jnp.concatenate(
            [
                (index == lane + k).astype(jnp.float32).astype(jnp.bfloat16)
                for k in range(0, total, LANES)
            ],
            axis=1,
        )
        held = jnp.dot(chosen, rows_ref[...], preferred_element_type=jnp.float32)
        squares = jnp.sum(held * held, axis=1, keepdims=True)
        unit_ref[pl.ds(start, block), :] = (held * lax.rsqrt(squares + 1e-06)).astype(jnp.bfloat16)

    pl.loop(0, 2)(step)


def own_pairs_kernel(side_ref, labels_ref, own_ref, best_ref, fold_ref):
    rows = own_ref.shape[0]
    labels = labels_ref[:, pl.ds(pl.multiple_of(side_ref[0] * rows, rows), rows)]
    down = down_lanes(labels)
    along = jnp.where(labels < 0, -3, labels)
    fold_ref[...] = jnp.full(fold_ref.shape, -1.0, jnp.float32)
    for start in range(0, rows, BLOCK):
        height = start + BLOCK
        scores = lax.dot_general(
            own_ref[pl.ds(0, height), :],
            own_ref[pl.ds(start, BLOCK), :],
            ROWS_BY_ROWS,
            preferred_element_type=jnp.float32,
        )
        keep = same_label(down[:height], along[:, start : start + BLOCK])
        row_id = lax.broadcasted_iota(jnp.int32, (height, BLOCK), 0)
        column_id = lax.broadcasted_iota(jnp.int32, (height, BLOCK), 1) + start
        kept = jnp.where(keep & (row_id != column_id), scores, -1.0)
        best_ref[:, pl.ds(start, BLOCK)] = jnp.max(kept, axis=0, keepdims=True)
        part = pl.ds(0, height)
        fold_ref[part, :] = jnp.maximum(fold_ref[part, :], fold_lanes(kept))
    best_ref[...] = jnp.maximum(best_ref[...], across(fold_ref[...]))


def cross_pairs_kernel(side_ref, labels_ref, own_ref, other_ref, own_best_ref, other_best_ref):
    rows = own_ref.shape[0]
    half = rows // 2
    side = side_ref[0]
    for turn in range(2):
        mine = pl.multiple_of((side ^ turn) * half, half)
        own_labels = labels_ref[:, pl.ds(pl.multiple_of(side * rows + mine, half), half)]
        other_labels = labels_ref[
            :, pl.ds(pl.multiple_of((1 - side) * rows + turn * half, half), half)
        ]
        down = down_lanes(own_labels)
        along = jnp.where(other_labels < 0, -3, other_labels)
        fold = jnp.full((half, LANES), -1.0, jnp.float32)
        for start in range(0, half, BLOCK):
            scores = lax.dot_general(
                own_ref[pl.ds(mine, half), :],
                other_ref[pl.ds(turn * half + start, BLOCK), :],
                ROWS_BY_ROWS,
                preferred_element_type=jnp.float32,
            )
            kept = jnp.where(same_label(down, along[:, start : start + BLOCK]), scores, -1.0)
            other_best_ref[:, pl.ds(turn * half + start, BLOCK)] = jnp.max(
                kept, axis=0, keepdims=True
            )
            fold = jnp.maximum(fold, fold_lanes(kept))
        own_best_ref[:, pl.ds(mine, half)] = across(fold)


def vmem():
    return pl.BlockSpec(memory_space=pltpu.VMEM)


def smem():
    return pl.BlockSpec(memory_space=pltpu.SMEM)


def per_device(embeddings, send_row, slot_cluster):
    rows, width = embeddings.shape
    side = lax.axis_index("grp").astype(jnp.int32).reshape(1)
    labels = slot_cluster.reshape(1, -1)
    best_shape = jax.ShapeDtypeStruct((1, rows), jnp.float32)
    params = pltpu.CompilerParams(vmem_limit_bytes=VMEM_LIMIT)

    unit = pl.pallas_call(
        unit_rows_kernel,
        out_shape=jax.ShapeDtypeStruct((rows, width), jnp.bfloat16),
        in_specs=[vmem(), vmem()],
        out_specs=vmem(),
        compiler_params=params,
        cost_estimate=pl.CostEstimate(
            flops=2 * rows * rows * width, bytes_accessed=4 * rows * width, transcendentals=rows
        ),
        name="unit_rows",
    )(send_row, embeddings)

    own = lax.all_to_all(unit, ("shard", "grp"), split_axis=0, concat_axis=0, tiled=True)
    other = lax.ppermute(own, "grp", [(0, 1), (1, 0)])

    own_best = pl.pallas_call(
        own_pairs_kernel,
        out_shape=best_shape,
        in_specs=[smem(), vmem(), vmem()],
        out_specs=vmem(),
        scratch_shapes=[pltpu.VMEM((rows, LANES), jnp.float32)],
        compiler_params=params,
        cost_estimate=pl.CostEstimate(
            flops=rows * rows * width, bytes_accessed=2 * rows * width, transcendentals=0
        ),
        name="own_pairs",
    )(side, labels, own)

    cross_best, other_best = pl.pallas_call(
        cross_pairs_kernel,
        out_shape=[best_shape, best_shape],
        in_specs=[smem(), vmem(), vmem(), vmem()],
        out_specs=[vmem(), vmem()],
        compiler_params=params,
        cost_estimate=pl.CostEstimate(
            flops=rows * rows * width, bytes_accessed=4 * rows * width, transcendentals=0
        ),
        name="cross_pairs",
    )(side, labels, own, other)

    returned = lax.ppermute(other_best, "grp", [(0, 1), (1, 0)])
    best = jnp.maximum(jnp.maximum(own_best, cross_best), returned)
    return best.reshape(rows)


def solution(mesh):
    placed = (P(("shard", "grp"), None), P(("shard", "grp"), None), P("shard"))
    return jax.shard_map(
        per_device, mesh=mesh, in_specs=placed, out_specs=P(("shard", "grp")), check_vma=False
    )
```

```python
import jax
import jax.numpy as jnp
from jax import lax
from jax.experimental import pallas as pl
from jax.experimental.pallas import tpu as pltpu
from jax.sharding import PartitionSpec as P

LANES = 128
SUBLANES = 8
STRIDE = SUBLANES + 1
BLOCK = 256
PARTS = 2
SPAN = 1024
UNROLL = 128
ROWS_BY_ROWS = (((1,), (1,)), ((), ()))


def down_lanes(row):
    parts = [
        jnp.transpose(jnp.broadcast_to(row[:, j : j + LANES], (LANES, LANES)))
        for j in range(0, row.shape[1], LANES)
    ]
    return jnp.concatenate(parts, axis=0)


def fold_lanes(values):
    best = values[:, :LANES]
    for j in range(LANES, values.shape[1], LANES):
        best = jnp.maximum(best, values[:, j : j + LANES])
    return best


def across(values):
    parts = [
        jnp.max(jnp.transpose(values[i : i + LANES]), axis=0, keepdims=True)
        for i in range(0, values.shape[0], LANES)
    ]
    return jnp.concatenate(parts, axis=0)


def along_lanes(row):
    return jnp.concatenate([row[:, j : j + LANES] for j in range(0, row.shape[1], LANES)], axis=0)


def same_label(down, labels):
    return jnp.concatenate(
        [down == labels[:, j : j + LANES] for j in range(0, labels.shape[1], LANES)], axis=1
    )


def unit_rows_kernel(
    index_ref,
    rows_ref,
    unit_ref,
    rows_buf,
    unit_buf,
    source,
    target,
    squares,
    index_buf,
    place_buf,
    place_smem,
    index_sem,
    place_sem,
    in_sem,
    out_sem,
):
    rows, width = rows_ref.shape
    tiles = width // LANES
    group_in = (tiles + 1) * STRIDE
    group_out = tiles * STRIDE
    part = rows // PARTS

    def copy_in(p):
        span = pl.ds(p * part, part)
        return pltpu.make_async_copy(rows_ref.at[span, :], rows_buf.at[span, :], in_sem.at[p])

    def copy_out(p):
        span = pl.ds(p * part, part)
        return pltpu.make_async_copy(unit_buf.at[span, :], unit_ref.at[span, :], out_sem.at[p])

    copy_index = pltpu.make_async_copy(index_ref, index_buf, index_sem)
    copy_index.start()
    for p in range(PARTS):
        copy_in(p).start()
    empty = rows // SUBLANES * group_in
    source[pl.ds(empty, group_in), :] = jnp.zeros((group_in, LANES), jnp.float32)
    copy_place = pltpu.make_async_copy(place_buf, place_smem, place_sem)

    for p in range(PARTS):
        copy_in(p).wait()

        @pl.loop(0, part // UNROLL)
        def _(c):
            first = p * part + c * UNROLL
            held = rows_buf[pl.ds(pl.multiple_of(first, UNROLL), UNROLL), :].astype(jnp.float32)
            total = jnp.zeros((UNROLL, LANES), jnp.float32)
            for j in range(tiles):
                piece = held[:, j * LANES : (j + 1) * LANES]
                total = total + piece * piece
                for i in range(UNROLL // SUBLANES):
                    start = (first // SUBLANES + i) * group_in + j * STRIDE
                    source[pl.ds(start, SUBLANES), :] = piece[i * SUBLANES : (i + 1) * SUBLANES]
            squares[pl.ds(pl.multiple_of(first, UNROLL), UNROLL), :] = total

        if p == 0:
            copy_index.wait()
            index = index_buf[...]
            place_buf[...] = jnp.where(
                index < 0, empty, index + (index >> 3) * (group_in - SUBLANES)
            )
            copy_place.start()

    total = jnp.dot(
        squares[...],
        jnp.ones((LANES, LANES), jnp.float32),
        preferred_element_type=jnp.float32,
        precision=lax.Precision.HIGHEST,
    )
    scale = lax.rsqrt(total + 1e-06)
    for i in range(rows // SUBLANES):
        start = i * group_in + tiles * STRIDE
        source[pl.ds(start, SUBLANES), :] = scale[i * SUBLANES : (i + 1) * SUBLANES]
    copy_place.wait()

    for p in range(PARTS):

        @pl.loop(0, part // UNROLL)
        def _(c):
            first = p * part + c * UNROLL
            base = first // SUBLANES * group_out
            for s in range(UNROLL):
                place = place_smem[0, first + s]
                row = source[pl.ds(place, tiles, stride=STRIDE), :]
                scale = source[pl.ds(place + tiles * STRIDE, 1), :]
                start = base + s // SUBLANES * group_out + s % SUBLANES
                target[pl.ds(start, tiles, stride=STRIDE), :] = row * scale

        @pl.loop(0, part // UNROLL)
        def _(c):
            first = p * part + c * UNROLL
            base = first // SUBLANES * group_out
            groups = [
                jnp.concatenate(
                    [
                        target[pl.ds(base + i * group_out + j * STRIDE, SUBLANES), :]
                        for j in range(tiles)
                    ],
                    axis=1,
                )
                for i in range(UNROLL // SUBLANES)
            ]
            unit_buf[pl.ds(pl.multiple_of(first, UNROLL), UNROLL), :] = jnp.concatenate(
                groups, axis=0
            ).astype(jnp.bfloat16)

        copy_out(p).start()
    for p in range(PARTS):
        copy_out(p).wait()


def own_pairs_kernel(side_ref, labels_ref, own_hbm, best_ref, own_ref, fold_ref, sem):
    rows = own_ref.shape[0]
    copies = [
        pltpu.make_async_copy(
            own_hbm.at[pl.ds(start, SPAN), :], own_ref.at[pl.ds(start, SPAN), :], sem.at[i]
        )
        for i, start in enumerate(range(0, rows, SPAN))
    ]
    for copy in copies:
        copy.start()
    labels = labels_ref[:, pl.ds(pl.multiple_of(side_ref[0] * rows, rows), rows)]
    down = down_lanes(labels)
    along = jnp.where(labels < 0, -3, labels)
    fold_ref[...] = jnp.full(fold_ref.shape, -1.0, jnp.float32)
    columns = []
    for start in range(0, rows, BLOCK):
        if start % SPAN == 0:
            copies[start // SPAN].wait()
        height = start + BLOCK
        scores = lax.dot_general(
            own_ref[pl.ds(0, height), :],
            own_ref[pl.ds(start, BLOCK), :],
            ROWS_BY_ROWS,
            preferred_element_type=jnp.float32,
        )
        keep = same_label(down[:height], along[:, start : start + BLOCK])
        row_id = lax.broadcasted_iota(jnp.int32, (height, BLOCK), 0)
        column_id = lax.broadcasted_iota(jnp.int32, (height, BLOCK), 1) + start
        kept = jnp.where(keep & (row_id != column_id), scores, -1.0)
        columns.append(along_lanes(jnp.max(kept, axis=0, keepdims=True)))
        part = pl.ds(0, height)
        fold_ref[part, :] = jnp.maximum(fold_ref[part, :], fold_lanes(kept))
    best_ref[...] = jnp.maximum(jnp.concatenate(columns, axis=0), across(fold_ref[...]))


def cross_pairs_kernel(
    side_ref, labels_ref, best_ref, own_ref, other_hbm, own_best_ref, other_best_ref, other_ref, sem
):
    rows = own_ref.shape[0]
    half = rows // 2
    tiles = half // LANES
    side = side_ref[0]
    copies = [
        pltpu.make_async_copy(
            other_hbm.at[pl.ds(start, half), :], other_ref.at[pl.ds(start, half), :], sem.at[i]
        )
        for i, start in enumerate(range(0, rows, half))
    ]
    for copy in copies:
        copy.start()
    for turn in range(2):
        mine = side ^ turn
        first = pl.multiple_of(mine * half, half)
        own_labels = labels_ref[:, pl.ds(pl.multiple_of(side * rows + first, half), half)]
        other_labels = labels_ref[
            :, pl.ds(pl.multiple_of((1 - side) * rows + turn * half, half), half)
        ]
        down = down_lanes(own_labels)
        along = jnp.where(other_labels < 0, -3, other_labels)
        fold = jnp.full((half, LANES), -1.0, jnp.float32)
        columns = []
        copies[turn].wait()
        for start in range(0, half, BLOCK):
            scores = lax.dot_general(
                own_ref[pl.ds(first, half), :],
                other_ref[pl.ds(turn * half + start, BLOCK), :],
                ROWS_BY_ROWS,
                preferred_element_type=jnp.float32,
            )
            kept = jnp.where(same_label(down, along[:, start : start + BLOCK]), scores, -1.0)
            columns.append(along_lanes(jnp.max(kept, axis=0, keepdims=True)))
            fold = jnp.maximum(fold, fold_lanes(kept))
        other_best_ref[pl.ds(turn * tiles, tiles), :] = jnp.concatenate(columns, axis=0)
        part = pl.ds(pl.multiple_of(mine * tiles, tiles), tiles)
        own_best_ref[part, :] = jnp.maximum(best_ref[part, :], across(fold))


def vmem():
    return pl.BlockSpec(memory_space=pltpu.VMEM)


def smem():
    return pl.BlockSpec(memory_space=pltpu.SMEM)


def anywhere():
    return pl.BlockSpec(memory_space=pl.ANY)


def per_device(embeddings, send_row, slot_cluster):
    rows, width = embeddings.shape
    tiles = width // LANES
    groups = rows // SUBLANES
    side = lax.axis_index("grp").astype(jnp.int32).reshape(1)
    labels = slot_cluster.reshape(1, -1)
    row_shape = jax.ShapeDtypeStruct((rows, width), jnp.bfloat16)
    best_shape = jax.ShapeDtypeStruct((rows // LANES, LANES), jnp.float32)

    unit = pl.pallas_call(
        unit_rows_kernel,
        out_shape=row_shape,
        in_specs=[anywhere(), anywhere()],
        out_specs=anywhere(),
        scratch_shapes=[
            pltpu.VMEM((rows, width), jnp.bfloat16),
            pltpu.VMEM((rows, width), jnp.bfloat16),
            pltpu.VMEM(((groups + 1) * (tiles + 1) * STRIDE, LANES), jnp.float32),
            pltpu.VMEM((groups * tiles * STRIDE, LANES), jnp.float32),
            pltpu.VMEM((rows, LANES), jnp.float32),
            pltpu.VMEM((1, rows), jnp.int32),
            pltpu.VMEM((1, rows), jnp.int32),
            pltpu.SMEM((1, rows), jnp.int32),
            pltpu.SemaphoreType.DMA,
            pltpu.SemaphoreType.DMA,
            pltpu.SemaphoreType.DMA((PARTS,)),
            pltpu.SemaphoreType.DMA((PARTS,)),
        ],
        compiler_params=pltpu.CompilerParams(vmem_limit_bytes=60 << 20),
        cost_estimate=pl.CostEstimate(
            flops=8 * rows * width, bytes_accessed=4 * rows * width, transcendentals=rows
        ),
        name="unit_rows",
    )(send_row, embeddings)

    own = lax.all_to_all(unit, ("shard", "grp"), split_axis=0, concat_axis=0, tiled=True)
    other = lax.ppermute(own, "grp", [(0, 1), (1, 0)])

    own_best, own_kept = pl.pallas_call(
        own_pairs_kernel,
        out_shape=[best_shape, row_shape],
        in_specs=[smem(), vmem(), anywhere()],
        out_specs=[vmem(), vmem()],
        scratch_shapes=[
            pltpu.VMEM((rows, LANES), jnp.float32),
            pltpu.SemaphoreType.DMA((rows // SPAN,)),
        ],
        compiler_params=pltpu.CompilerParams(vmem_limit_bytes=26 << 20),
        cost_estimate=pl.CostEstimate(
            flops=rows * rows * width, bytes_accessed=2 * rows * width, transcendentals=0
        ),
        name="own_pairs",
    )(side, labels, own)

    own_best, other_best = pl.pallas_call(
        cross_pairs_kernel,
        out_shape=[best_shape, best_shape],
        in_specs=[smem(), vmem(), vmem(), vmem(), anywhere()],
        out_specs=[vmem(), vmem()],
        scratch_shapes=[
            pltpu.VMEM((rows, width), jnp.bfloat16),
            pltpu.SemaphoreType.DMA((2,)),
        ],
        compiler_params=pltpu.CompilerParams(vmem_limit_bytes=26 << 20),
        cost_estimate=pl.CostEstimate(
            flops=rows * rows * width, bytes_accessed=4 * rows * width, transcendentals=0
        ),
        name="cross_pairs",
    )(side, labels, own_best, own_kept, other)

    returned = lax.ppermute(other_best, "grp", [(0, 1), (1, 0)])
    return jnp.maximum(own_best, returned).reshape(rows)


def solution(mesh):
    placed = (P(("shard", "grp"), None), P(("shard", "grp"), None), P("shard"))
    return jax.shard_map(
        per_device, mesh=mesh, in_specs=placed, out_specs=P(("shard", "grp")), check_vma=False
    )
```

```python
import jax
import jax.numpy as jnp
from jax import lax
from jax.experimental import pallas as pl
from jax.experimental.pallas import tpu as pltpu
from jax.sharding import PartitionSpec as P

LANES = 128
SUBLANES = 8
STRIDE = SUBLANES + 1
BLOCK = 256
PARTS = 4
SPAN = 1024
UNROLL = 128
ROWS_BY_ROWS = (((1,), (1,)), ((), ()))


def down_lanes(row):
    parts = [
        jnp.transpose(jnp.broadcast_to(row[:, j : j + LANES], (LANES, LANES)))
        for j in range(0, row.shape[1], LANES)
    ]
    return jnp.concatenate(parts, axis=0)


def fold_lanes(values):
    best = values[:, :LANES]
    for j in range(LANES, values.shape[1], LANES):
        best = jnp.maximum(best, values[:, j : j + LANES])
    return best


def across(values):
    parts = [
        jnp.max(jnp.transpose(values[i : i + LANES]), axis=0, keepdims=True)
        for i in range(0, values.shape[0], LANES)
    ]
    return jnp.concatenate(parts, axis=0)


def along_lanes(row):
    return jnp.concatenate([row[:, j : j + LANES] for j in range(0, row.shape[1], LANES)], axis=0)


def add_lanes(values):
    terms = []
    for _ in range(3):
        term = values.astype(jnp.bfloat16)
        terms.append(term)
        values = values - term.astype(jnp.float32)
    ones = jnp.ones((3 * LANES, LANES), jnp.bfloat16)
    return jnp.dot(jnp.concatenate(terms, axis=1), ones, preferred_element_type=jnp.float32)


def unit_rows_kernel(
    index_ref,
    rows_ref,
    unit_ref,
    rows_buf,
    source,
    target,
    squares,
    index_buf,
    place_buf,
    place_smem,
    index_sem,
    place_sem,
    in_sem,
):
    rows, width = rows_ref.shape
    tiles = width // LANES
    group_in = (tiles + 1) * STRIDE
    group_out = tiles * STRIDE
    part = rows // PARTS

    def copy_in(p):
        span = pl.ds(p * part, part)
        return pltpu.make_async_copy(rows_ref.at[span, :], rows_buf.at[span, :], in_sem.at[p])

    copy_index = pltpu.make_async_copy(index_ref, index_buf, index_sem)
    copy_index.start()
    for p in range(PARTS):
        copy_in(p).start()
    empty = rows // SUBLANES * group_in
    source[pl.ds(empty, group_in), :] = jnp.zeros((group_in, LANES), jnp.float32)
    copy_place = pltpu.make_async_copy(place_buf, place_smem, place_sem)

    for p in range(PARTS):
        copy_in(p).wait()

        @pl.loop(0, part // UNROLL)
        def _(c):
            first = pl.multiple_of(p * part + c * UNROLL, UNROLL)
            held = rows_buf[pl.ds(first, UNROLL), :].astype(jnp.float32)
            total = jnp.zeros((UNROLL, LANES), jnp.float32)
            for j in range(tiles):
                piece = held[:, j * LANES : (j + 1) * LANES]
                total = total + piece * piece
                for i in range(UNROLL // SUBLANES):
                    start = (first // SUBLANES + i) * group_in + j * STRIDE
                    source[pl.ds(start, SUBLANES), :] = piece[i * SUBLANES : (i + 1) * SUBLANES]
            squares[pl.ds(first, UNROLL), :] = total

        if p == 0:
            copy_index.wait()
            index = index_buf[...]
            place_buf[...] = jnp.where(
                index < 0, empty, index + (index >> 3) * (group_in - SUBLANES)
            )
            copy_place.start()

    scale = lax.rsqrt(add_lanes(squares[...]) + 1e-06)
    for i in range(rows // SUBLANES):
        start = i * group_in + tiles * STRIDE
        source[pl.ds(start, SUBLANES), :] = scale[i * SUBLANES : (i + 1) * SUBLANES]
    copy_place.wait()

    def move(first):
        base = first // SUBLANES * group_out
        for s in range(UNROLL):
            place = place_smem[0, first + s]
            row = source[pl.ds(place, tiles, stride=STRIDE), :]
            factor = source[pl.ds(place + tiles * STRIDE, 1), :]
            start = base + s // SUBLANES * group_out + s % SUBLANES
            target[pl.ds(start, tiles, stride=STRIDE), :] = row * factor

    def write(first):
        base = first // SUBLANES * group_out
        groups = []
        for i in range(UNROLL // SUBLANES):
            start = base + i * group_out
            pieces = [target[pl.ds(start + j * STRIDE, SUBLANES), :] for j in range(tiles)]
            groups.append(jnp.concatenate(pieces, axis=1))
        unit_ref[pl.ds(pl.multiple_of(first, UNROLL), UNROLL), :] = jnp.concatenate(
            groups, axis=0
        ).astype(jnp.bfloat16)

    move(0)

    @pl.loop(1, rows // UNROLL)
    def _(c):
        write((c - 1) * UNROLL)
        move(c * UNROLL)

    write(rows - UNROLL)


def matched(left, right, down, along):
    scores = lax.dot_general(left, right, ROWS_BY_ROWS, preferred_element_type=jnp.float32)
    keep = [down == along[:, j : j + LANES] for j in range(0, along.shape[1], LANES)]
    return jnp.where(jnp.concatenate(keep, axis=1), scores, -1.0)


def own_column(own_ref, down, along, start):
    height = start + BLOCK
    kept = matched(
        own_ref[pl.ds(0, height), :],
        own_ref[pl.ds(start, BLOCK), :],
        down[:height],
        along[:, start : start + BLOCK],
    )
    row_id = lax.broadcasted_iota(jnp.int32, (height, BLOCK), 0)
    column_id = lax.broadcasted_iota(jnp.int32, (height, BLOCK), 1) + start
    return jnp.where(row_id != column_id, kept, -1.0)


def own_pairs_kernel(side_ref, labels_ref, own_hbm, best_ref, own_ref, fold_ref, sem):
    rows = own_ref.shape[0]
    copies = [
        pltpu.make_async_copy(
            own_hbm.at[pl.ds(start, SPAN), :], own_ref.at[pl.ds(start, SPAN), :], sem.at[i]
        )
        for i, start in enumerate(range(0, rows, SPAN))
    ]
    for copy in copies:
        copy.start()
    labels = labels_ref[:, pl.ds(pl.multiple_of(side_ref[0] * rows, rows), rows)]
    down = down_lanes(labels)
    along = jnp.where(labels < 0, -3, labels)
    fold_ref[...] = jnp.full(fold_ref.shape, -1.0, jnp.float32)
    columns = []
    for start in range(0, rows, BLOCK):
        if start % SPAN == 0:
            copies[start // SPAN].wait()
        kept = own_column(own_ref, down, along, start)
        columns.append(along_lanes(jnp.max(kept, axis=0, keepdims=True)))
        part = pl.ds(0, start + BLOCK)
        fold_ref[part, :] = jnp.maximum(fold_ref[part, :], fold_lanes(kept))
    best_ref[...] = jnp.maximum(jnp.concatenate(columns, axis=0), across(fold_ref[...]))


def cross_pairs_kernel(
    side_ref, labels_ref, best_ref, own_ref, other_hbm, own_best_ref, other_best_ref, other_ref, sem
):
    rows = own_ref.shape[0]
    half = rows // 2
    tiles = half // LANES
    side = side_ref[0]
    copies = [
        pltpu.make_async_copy(
            other_hbm.at[pl.ds(start, half), :], other_ref.at[pl.ds(start, half), :], sem.at[i]
        )
        for i, start in enumerate(range(0, rows, half))
    ]
    for copy in copies:
        copy.start()

    for turn in range(2):
        mine = side ^ turn
        first = pl.multiple_of(mine * half, half)
        own_labels = labels_ref[:, pl.ds(pl.multiple_of(side * rows + first, half), half)]
        other_labels = labels_ref[
            :, pl.ds(pl.multiple_of((1 - side) * rows + turn * half, half), half)
        ]
        down = down_lanes(own_labels)
        along = jnp.where(other_labels < 0, -3, other_labels)
        fold = jnp.full((half, LANES), -1.0, jnp.float32)
        columns = []
        copies[turn].wait()
        for start in range(0, half, BLOCK):
            kept = matched(
                own_ref[pl.ds(first, half), :],
                other_ref[pl.ds(turn * half + start, BLOCK), :],
                down,
                along[:, start : start + BLOCK],
            )
            columns.append(along_lanes(jnp.max(kept, axis=0, keepdims=True)))
            fold = jnp.maximum(fold, fold_lanes(kept))
        other_best_ref[pl.ds(turn * tiles, tiles), :] = jnp.concatenate(columns, axis=0)
        part = pl.ds(pl.multiple_of(mine * tiles, tiles), tiles)
        own_best_ref[part, :] = jnp.maximum(best_ref[part, :], across(fold))


def vmem():
    return pl.BlockSpec(memory_space=pltpu.VMEM)


def smem():
    return pl.BlockSpec(memory_space=pltpu.SMEM)


def anywhere():
    return pl.BlockSpec(memory_space=pl.ANY)


def per_device(embeddings, send_row, slot_cluster):
    rows, width = embeddings.shape
    tiles = width // LANES
    groups = rows // SUBLANES
    side = lax.axis_index("grp").astype(jnp.int32).reshape(1)
    labels = slot_cluster.reshape(1, -1)
    row_shape = jax.ShapeDtypeStruct((rows, width), jnp.bfloat16)
    best_shape = jax.ShapeDtypeStruct((rows // LANES, LANES), jnp.float32)

    unit = pl.pallas_call(
        unit_rows_kernel,
        out_shape=pltpu.VMEM((rows, width), jnp.bfloat16),
        in_specs=[anywhere(), anywhere()],
        out_specs=vmem(),
        scratch_shapes=[
            pltpu.VMEM((rows, width), jnp.bfloat16),
            pltpu.VMEM(((groups + 1) * (tiles + 1) * STRIDE, LANES), jnp.float32),
            pltpu.VMEM((groups * tiles * STRIDE, LANES), jnp.float32),
            pltpu.VMEM((rows, LANES), jnp.float32),
            pltpu.VMEM((1, rows), jnp.int32),
            pltpu.VMEM((1, rows), jnp.int32),
            pltpu.SMEM((1, rows), jnp.int32),
            pltpu.SemaphoreType.DMA,
            pltpu.SemaphoreType.DMA,
            pltpu.SemaphoreType.DMA((PARTS,)),
        ],
        compiler_params=pltpu.CompilerParams(vmem_limit_bytes=59 << 20),
        cost_estimate=pl.CostEstimate(
            flops=8 * rows * width, bytes_accessed=4 * rows * width, transcendentals=rows
        ),
        name="unit_rows",
    )(send_row, embeddings)

    own = lax.all_to_all(unit, ("shard", "grp"), split_axis=0, concat_axis=0, tiled=True)
    other = lax.ppermute(own, "grp", [(0, 1), (1, 0)])

    own_best, own_kept = pl.pallas_call(
        own_pairs_kernel,
        out_shape=[best_shape, row_shape],
        in_specs=[smem(), vmem(), anywhere()],
        out_specs=[vmem(), vmem()],
        scratch_shapes=[
            pltpu.VMEM((rows, LANES), jnp.float32),
            pltpu.SemaphoreType.DMA((rows // SPAN,)),
        ],
        compiler_params=pltpu.CompilerParams(vmem_limit_bytes=26 << 20),
        cost_estimate=pl.CostEstimate(
            flops=rows * rows * width, bytes_accessed=2 * rows * width, transcendentals=0
        ),
        name="own_pairs",
    )(side, labels, own)

    own_best, other_best = pl.pallas_call(
        cross_pairs_kernel,
        out_shape=[best_shape, best_shape],
        in_specs=[smem(), vmem(), vmem(), vmem(), anywhere()],
        out_specs=[vmem(), vmem()],
        scratch_shapes=[
            pltpu.VMEM((rows, width), jnp.bfloat16),
            pltpu.SemaphoreType.DMA((2,)),
        ],
        compiler_params=pltpu.CompilerParams(vmem_limit_bytes=26 << 20),
        cost_estimate=pl.CostEstimate(
            flops=rows * rows * width, bytes_accessed=4 * rows * width, transcendentals=0
        ),
        name="cross_pairs",
    )(side, labels, own_best, own_kept, other)

    returned = lax.ppermute(other_best, "grp", [(0, 1), (1, 0)])
    return jnp.maximum(own_best, returned).reshape(rows)


def solution(mesh):
    placed = (P(("shard", "grp"), None), P(("shard", "grp"), None), P("shard"))
    return jax.shard_map(
        per_device, mesh=mesh, in_specs=placed, out_specs=P(("shard", "grp")), check_vma=False
    )
```

```python
import jax
import jax.numpy as jnp
from jax import lax
from jax.experimental import pallas as pl
from jax.experimental.pallas import tpu as pltpu
from jax.sharding import PartitionSpec as P

LANES = 128
SUBLANES = 8
STRIDE = SUBLANES + 1
BLOCK = 256
PARTS = 4
OWN_WAITS = {0: 2, 2: 8}
CROSS_WAITS = {0: 2, 2: 8}
UNROLL = 128
ROWS_BY_ROWS = (((1,), (1,)), ((), ()))


def down_lanes(row):
    parts = [
        jnp.transpose(jnp.broadcast_to(row[:, j : j + LANES], (LANES, LANES)))
        for j in range(0, row.shape[1], LANES)
    ]
    return jnp.concatenate(parts, axis=0)


def fold_lanes(values):
    best = values[:, :LANES]
    for j in range(LANES, values.shape[1], LANES):
        best = jnp.maximum(best, values[:, j : j + LANES])
    return best


def across(values):
    parts = [
        jnp.max(jnp.transpose(values[i : i + LANES]), axis=0, keepdims=True)
        for i in range(0, values.shape[0], LANES)
    ]
    return jnp.concatenate(parts, axis=0)


def along_lanes(row):
    return jnp.concatenate([row[:, j : j + LANES] for j in range(0, row.shape[1], LANES)], axis=0)


def add_lanes(values):
    terms = []
    for _ in range(3):
        term = values.astype(jnp.bfloat16)
        terms.append(term)
        values = values - term.astype(jnp.float32)
    ones = jnp.ones((3 * LANES, LANES), jnp.bfloat16)
    return jnp.dot(jnp.concatenate(terms, axis=1), ones, preferred_element_type=jnp.float32)


def unit_rows_kernel(
    index_ref,
    rows_ref,
    unit_ref,
    rows_buf,
    source,
    target,
    squares,
    index_buf,
    place_buf,
    place_smem,
    index_sem,
    place_sem,
    in_sem,
):
    rows, width = rows_ref.shape
    tiles = width // LANES
    group_in = (tiles + 1) * STRIDE
    group_out = tiles * STRIDE
    part = rows // PARTS

    def copy_in(p):
        span = pl.ds(p * part, part)
        return pltpu.make_async_copy(rows_ref.at[span, :], rows_buf.at[span, :], in_sem.at[p])

    copy_index = pltpu.make_async_copy(index_ref, index_buf, index_sem)
    copy_index.start()
    for p in range(PARTS):
        copy_in(p).start()
    empty = rows // SUBLANES * group_in
    source[pl.ds(empty, group_in), :] = jnp.zeros((group_in, LANES), jnp.float32)
    copy_place = pltpu.make_async_copy(place_buf, place_smem, place_sem)

    for p in range(PARTS):
        copy_in(p).wait()

        @pl.loop(0, part // UNROLL)
        def _(c):
            first = pl.multiple_of(p * part + c * UNROLL, UNROLL)
            held = rows_buf[pl.ds(first, UNROLL), :].astype(jnp.float32)
            total = jnp.zeros((UNROLL, LANES), jnp.float32)
            for j in range(tiles):
                piece = held[:, j * LANES : (j + 1) * LANES]
                total = total + piece * piece
                for i in range(UNROLL // SUBLANES):
                    start = (first // SUBLANES + i) * group_in + j * STRIDE
                    source[pl.ds(start, SUBLANES), :] = piece[i * SUBLANES : (i + 1) * SUBLANES]
            squares[pl.ds(first, UNROLL), :] = total

        if p == 0:
            copy_index.wait()
            index = index_buf[...]
            place_buf[...] = jnp.where(
                index < 0, empty, index + (index >> 3) * (group_in - SUBLANES)
            )
            copy_place.start()

    scale = lax.rsqrt(add_lanes(squares[...]) + 1e-06)
    for i in range(rows // SUBLANES):
        start = i * group_in + tiles * STRIDE
        source[pl.ds(start, SUBLANES), :] = scale[i * SUBLANES : (i + 1) * SUBLANES]
    copy_place.wait()

    def move(first):
        base = first // SUBLANES * group_out
        for s in range(UNROLL):
            place = place_smem[0, first + s]
            row = source[pl.ds(place, tiles, stride=STRIDE), :]
            factor = source[pl.ds(place + tiles * STRIDE, 1), :]
            start = base + s // SUBLANES * group_out + s % SUBLANES
            target[pl.ds(start, tiles, stride=STRIDE), :] = row * factor

    def write(first):
        base = first // SUBLANES * group_out
        groups = []
        for i in range(UNROLL // SUBLANES):
            start = base + i * group_out
            pieces = [target[pl.ds(start + j * STRIDE, SUBLANES), :] for j in range(tiles)]
            groups.append(jnp.concatenate(pieces, axis=1))
        unit_ref[pl.ds(pl.multiple_of(first, UNROLL), UNROLL), :] = jnp.concatenate(
            groups, axis=0
        ).astype(jnp.bfloat16)

    move(0)

    @pl.loop(1, rows // UNROLL)
    def _(c):
        write((c - 1) * UNROLL)
        move(c * UNROLL)

    write(rows - UNROLL)


def products(left, right):
    return lax.dot_general(left, right, ROWS_BY_ROWS, preferred_element_type=jnp.float32)


def matched(scores, down, along):
    keep = [down == along[:, j : j + LANES] for j in range(0, along.shape[1], LANES)]
    return jnp.where(jnp.concatenate(keep, axis=1), scores, -1.0)


def copies_in(source, target, sem):
    rows = target.shape[0]
    copies = [
        pltpu.make_async_copy(
            source.at[pl.ds(start, BLOCK), :], target.at[pl.ds(start, BLOCK), :], sem.at[i]
        )
        for i, start in enumerate(range(0, rows, BLOCK))
    ]
    for copy in copies:
        copy.start()
    return copies


def pipelined(score, reduce, copies, waits):
    scores = None
    for i in range(len(copies)):
        if i in waits:
            for copy in copies[i : waits[i]]:
                copy.wait()
        ahead = score(i * BLOCK)
        if scores is not None:
            reduce(scores, (i - 1) * BLOCK)
        scores = ahead
    reduce(scores, (len(copies) - 1) * BLOCK)


def own_pairs_kernel(side_ref, labels_ref, own_hbm, best_ref, own_ref, fold_ref, sem):
    rows = own_ref.shape[0]
    copies = copies_in(own_hbm, own_ref, sem)
    labels = labels_ref[:, pl.ds(pl.multiple_of(side_ref[0] * rows, rows), rows)]
    down = down_lanes(labels)
    along = jnp.where(labels < 0, -3, labels)
    fold_ref[...] = jnp.full(fold_ref.shape, -1.0, jnp.float32)
    columns = []

    def score(start):
        return products(own_ref[pl.ds(0, start + BLOCK), :], own_ref[pl.ds(start, BLOCK), :])

    def reduce(scores, start):
        height = start + BLOCK
        kept = matched(scores, down[:height], along[:, start : start + BLOCK])
        row_id = lax.broadcasted_iota(jnp.int32, (height, BLOCK), 0)
        column_id = lax.broadcasted_iota(jnp.int32, (height, BLOCK), 1) + start
        kept = jnp.where(row_id != column_id, kept, -1.0)
        columns.append(along_lanes(jnp.max(kept, axis=0, keepdims=True)))
        part = pl.ds(0, height)
        fold_ref[part, :] = jnp.maximum(fold_ref[part, :], fold_lanes(kept))

    pipelined(score, reduce, copies, OWN_WAITS)
    best_ref[...] = jnp.maximum(jnp.concatenate(columns, axis=0), across(fold_ref[...]))


def cross_pairs_kernel(
    side_ref, labels_ref, best_ref, own_ref, other_hbm, own_best_ref, other_best_ref, other_ref, sem
):
    rows = own_ref.shape[0]
    half = rows // 2
    tiles = half // LANES
    side = side_ref[0]
    copies = copies_in(other_hbm, other_ref, sem)
    firsts, downs, alongs = [], [], []
    for turn in range(2):
        first = pl.multiple_of((side ^ turn) * half, half)
        own_labels = labels_ref[:, pl.ds(pl.multiple_of(side * rows + first, half), half)]
        other_labels = labels_ref[
            :, pl.ds(pl.multiple_of((1 - side) * rows + turn * half, half), half)
        ]
        firsts.append(first)
        downs.append(down_lanes(own_labels))
        alongs.append(jnp.where(other_labels < 0, -3, other_labels))
    columns = []
    folds = [None, None]

    def score(start):
        first = firsts[start // half]
        return products(own_ref[pl.ds(first, half), :], other_ref[pl.ds(start, BLOCK), :])

    def reduce(scores, start):
        turn = start // half
        begin = start - turn * half
        kept = matched(scores, downs[turn], alongs[turn][:, begin : begin + BLOCK])
        columns.append(along_lanes(jnp.max(kept, axis=0, keepdims=True)))
        fold = fold_lanes(kept)
        folds[turn] = fold if folds[turn] is None else jnp.maximum(folds[turn], fold)

    pipelined(score, reduce, copies, CROSS_WAITS)
    other_best_ref[...] = jnp.concatenate(columns, axis=0)
    for turn in range(2):
        part = pl.ds(pl.multiple_of((side ^ turn) * tiles, tiles), tiles)
        own_best_ref[part, :] = jnp.maximum(best_ref[part, :], across(folds[turn]))


def vmem():
    return pl.BlockSpec(memory_space=pltpu.VMEM)


def smem():
    return pl.BlockSpec(memory_space=pltpu.SMEM)


def anywhere():
    return pl.BlockSpec(memory_space=pl.ANY)


def per_device(embeddings, send_row, slot_cluster):
    rows, width = embeddings.shape
    tiles = width // LANES
    groups = rows // SUBLANES
    side = lax.axis_index("grp").astype(jnp.int32).reshape(1)
    labels = slot_cluster.reshape(1, -1)
    row_shape = jax.ShapeDtypeStruct((rows, width), jnp.bfloat16)
    best_shape = jax.ShapeDtypeStruct((rows // LANES, LANES), jnp.float32)

    unit = pl.pallas_call(
        unit_rows_kernel,
        out_shape=pltpu.VMEM((rows, width), jnp.bfloat16),
        in_specs=[anywhere(), anywhere()],
        out_specs=vmem(),
        scratch_shapes=[
            pltpu.VMEM((rows, width), jnp.bfloat16),
            pltpu.VMEM(((groups + 1) * (tiles + 1) * STRIDE, LANES), jnp.float32),
            pltpu.VMEM((groups * tiles * STRIDE, LANES), jnp.float32),
            pltpu.VMEM((rows, LANES), jnp.float32),
            pltpu.VMEM((1, rows), jnp.int32),
            pltpu.VMEM((1, rows), jnp.int32),
            pltpu.SMEM((1, rows), jnp.int32),
            pltpu.SemaphoreType.DMA,
            pltpu.SemaphoreType.DMA,
            pltpu.SemaphoreType.DMA((PARTS,)),
        ],
        compiler_params=pltpu.CompilerParams(vmem_limit_bytes=59 << 20),
        cost_estimate=pl.CostEstimate(
            flops=8 * rows * width, bytes_accessed=4 * rows * width, transcendentals=rows
        ),
        name="unit_rows",
    )(send_row, embeddings)

    own = lax.all_to_all(unit, ("shard", "grp"), split_axis=0, concat_axis=0, tiled=True)
    other = lax.ppermute(own, "grp", [(0, 1), (1, 0)])

    own_best, own_kept = pl.pallas_call(
        own_pairs_kernel,
        out_shape=[best_shape, row_shape],
        in_specs=[smem(), vmem(), anywhere()],
        out_specs=[vmem(), vmem()],
        scratch_shapes=[
            pltpu.VMEM((rows, LANES), jnp.float32),
            pltpu.SemaphoreType.DMA((rows // BLOCK,)),
        ],
        compiler_params=pltpu.CompilerParams(vmem_limit_bytes=26 << 20),
        cost_estimate=pl.CostEstimate(
            flops=rows * rows * width, bytes_accessed=2 * rows * width, transcendentals=0
        ),
        name="own_pairs",
    )(side, labels, own)

    own_best, other_best = pl.pallas_call(
        cross_pairs_kernel,
        out_shape=[best_shape, best_shape],
        in_specs=[smem(), vmem(), vmem(), vmem(), anywhere()],
        out_specs=[vmem(), vmem()],
        scratch_shapes=[
            pltpu.VMEM((rows, width), jnp.bfloat16),
            pltpu.SemaphoreType.DMA((rows // BLOCK,)),
        ],
        compiler_params=pltpu.CompilerParams(vmem_limit_bytes=26 << 20),
        cost_estimate=pl.CostEstimate(
            flops=rows * rows * width, bytes_accessed=4 * rows * width, transcendentals=0
        ),
        name="cross_pairs",
    )(side, labels, own_best, own_kept, other)

    returned = lax.ppermute(other_best, "grp", [(0, 1), (1, 0)])
    return jnp.maximum(own_best, returned).reshape(rows)


def solution(mesh):
    placed = (P(("shard", "grp"), None), P(("shard", "grp"), None), P("shard"))
    return jax.shard_map(
        per_device, mesh=mesh, in_specs=placed, out_specs=P(("shard", "grp")), check_vma=False
    )
```

```python
import jax
import jax.numpy as jnp
from jax import lax
from jax.experimental import pallas as pl
from jax.experimental.pallas import tpu as pltpu
from jax.sharding import PartitionSpec as P

LANES = 128
SUBLANES = 8
STRIDE = SUBLANES + 1
BLOCK = 256
PARTS = 4
OWN_WAITS = {0: 2, 2: 8}
CROSS_WAITS = {0: 2, 2: 8}
UNROLL = 128
ROWS_BY_ROWS = (((1,), (1,)), ((), ()))


def down_lanes(row):
    parts = [
        jnp.transpose(jnp.broadcast_to(row[:, j : j + LANES], (LANES, LANES)))
        for j in range(0, row.shape[1], LANES)
    ]
    return jnp.concatenate(parts, axis=0)


def fold_lanes(values):
    best = values[:, :LANES]
    for j in range(LANES, values.shape[1], LANES):
        best = jnp.maximum(best, values[:, j : j + LANES])
    return best


def across(values):
    parts = [
        jnp.max(jnp.transpose(values[i : i + LANES]), axis=0, keepdims=True)
        for i in range(0, values.shape[0], LANES)
    ]
    return jnp.concatenate(parts, axis=0)


def along_lanes(row):
    return jnp.concatenate([row[:, j : j + LANES] for j in range(0, row.shape[1], LANES)], axis=0)


def add_lanes(values):
    terms = []
    for _ in range(3):
        term = values.astype(jnp.bfloat16)
        terms.append(term)
        values = values - term.astype(jnp.float32)
    ones = jnp.ones((3 * LANES, LANES), jnp.bfloat16)
    return jnp.dot(jnp.concatenate(terms, axis=1), ones, preferred_element_type=jnp.float32)


def unit_rows_kernel(
    index_ref,
    rows_ref,
    unit_ref,
    rows_buf,
    source,
    target,
    squares,
    index_buf,
    place_buf,
    place_smem,
    index_sem,
    place_sem,
    in_sem,
):
    rows, width = rows_ref.shape
    tiles = width // LANES
    group_in = (tiles + 1) * STRIDE
    group_out = tiles * STRIDE
    part = rows // PARTS

    def copy_in(p):
        span = pl.ds(p * part, part)
        return pltpu.make_async_copy(rows_ref.at[span, :], rows_buf.at[span, :], in_sem.at[p])

    copy_index = pltpu.make_async_copy(index_ref, index_buf, index_sem)
    copy_index.start()
    for p in range(PARTS):
        copy_in(p).start()
    empty = rows // SUBLANES * group_in
    source[pl.ds(empty, group_in), :] = jnp.zeros((group_in, LANES), jnp.float32)
    copy_place = pltpu.make_async_copy(place_buf, place_smem, place_sem)

    for p in range(PARTS):
        copy_in(p).wait()

        @pl.loop(0, part // UNROLL)
        def _(c):
            first = pl.multiple_of(p * part + c * UNROLL, UNROLL)
            held = rows_buf[pl.ds(first, UNROLL), :].astype(jnp.float32)
            total = jnp.zeros((UNROLL, LANES), jnp.float32)
            for j in range(tiles):
                piece = held[:, j * LANES : (j + 1) * LANES]
                total = total + piece * piece
                for i in range(UNROLL // SUBLANES):
                    start = (first // SUBLANES + i) * group_in + j * STRIDE
                    source[pl.ds(start, SUBLANES), :] = piece[i * SUBLANES : (i + 1) * SUBLANES]
            squares[pl.ds(first, UNROLL), :] = total

        if p == 0:
            copy_index.wait()
            index = index_buf[...]
            place_buf[...] = jnp.where(
                index < 0, empty, index + (index >> 3) * (group_in - SUBLANES)
            )
            copy_place.start()

    scale = lax.rsqrt(add_lanes(squares[...]) + 1e-06)
    for i in range(rows // SUBLANES):
        start = i * group_in + tiles * STRIDE
        source[pl.ds(start, SUBLANES), :] = scale[i * SUBLANES : (i + 1) * SUBLANES]
    copy_place.wait()

    def move(first):
        base = first // SUBLANES * group_out
        for s in range(UNROLL):
            place = place_smem[0, first + s]
            row = source[pl.ds(place, tiles, stride=STRIDE), :]
            factor = source[pl.ds(place + tiles * STRIDE, 1), :]
            start = base + s // SUBLANES * group_out + s % SUBLANES
            target[pl.ds(start, tiles, stride=STRIDE), :] = row * factor

    def write(first):
        base = first // SUBLANES * group_out
        groups = []
        for i in range(UNROLL // SUBLANES):
            start = base + i * group_out
            pieces = [target[pl.ds(start + j * STRIDE, SUBLANES), :] for j in range(tiles)]
            groups.append(jnp.concatenate(pieces, axis=1))
        unit_ref[pl.ds(pl.multiple_of(first, UNROLL), UNROLL), :] = jnp.concatenate(
            groups, axis=0
        ).astype(jnp.bfloat16)

    move(0)

    @pl.loop(1, rows // UNROLL)
    def _(c):
        write((c - 1) * UNROLL)
        move(c * UNROLL)

    write(rows - UNROLL)


def products(left, right):
    return lax.dot_general(left, right, ROWS_BY_ROWS, preferred_element_type=jnp.float32)


def matched(scores, down, along):
    keep = [down == along[:, j : j + LANES] for j in range(0, along.shape[1], LANES)]
    return jnp.where(jnp.concatenate(keep, axis=1), scores, -1.0)


def copies_in(source, target, sem):
    rows = target.shape[0]
    copies = [
        pltpu.make_async_copy(
            source.at[pl.ds(start, BLOCK), :], target.at[pl.ds(start, BLOCK), :], sem.at[i]
        )
        for i, start in enumerate(range(0, rows, BLOCK))
    ]
    for copy in copies:
        copy.start()
    return copies


def pipelined(score, reduce, copies, waits):
    scores = None
    for i in range(len(copies)):
        if i in waits:
            for copy in copies[i : waits[i]]:
                copy.wait()
        ahead = score(i * BLOCK)
        if scores is not None:
            reduce(scores, (i - 1) * BLOCK)
        scores = ahead
    reduce(scores, (len(copies) - 1) * BLOCK)


def own_pairs_kernel(side_ref, labels_ref, own_hbm, best_ref, own_ref, fold_ref, sem):
    rows = own_ref.shape[0]
    copies = copies_in(own_hbm, own_ref, sem)
    labels = labels_ref[:, pl.ds(pl.multiple_of(side_ref[0] * rows, rows), rows)]
    down = down_lanes(labels)
    along = jnp.where(labels < 0, -3, labels)
    fold_ref[...] = jnp.full(fold_ref.shape, -1.0, jnp.float32)
    columns = []

    def score(start):
        return products(own_ref[pl.ds(0, start + BLOCK), :], own_ref[pl.ds(start, BLOCK), :])

    def reduce(scores, start):
        height = start + BLOCK
        kept = matched(scores, down[:height], along[:, start : start + BLOCK])
        row_id = lax.broadcasted_iota(jnp.int32, (height, BLOCK), 0)
        column_id = lax.broadcasted_iota(jnp.int32, (height, BLOCK), 1) + start
        kept = jnp.where(row_id != column_id, kept, -1.0)
        columns.append(along_lanes(jnp.max(kept, axis=0, keepdims=True)))
        part = pl.ds(0, height)
        fold_ref[part, :] = jnp.maximum(fold_ref[part, :], fold_lanes(kept))

    pipelined(score, reduce, copies, OWN_WAITS)
    best_ref[...] = jnp.maximum(jnp.concatenate(columns, axis=0), across(fold_ref[...]))


def cross_pairs_kernel(
    side_ref, labels_ref, best_ref, own_ref, other_hbm, own_best_ref, other_best_ref, other_ref, sem
):
    rows = own_ref.shape[0]
    half = rows // 2
    tiles = half // LANES
    side = side_ref[0]
    copies = copies_in(other_hbm, other_ref, sem)
    firsts, downs, alongs = [], [], []
    for turn in range(2):
        first = pl.multiple_of((side ^ turn) * half, half)
        own_labels = labels_ref[:, pl.ds(pl.multiple_of(side * rows + first, half), half)]
        other_labels = labels_ref[
            :, pl.ds(pl.multiple_of((1 - side) * rows + turn * half, half), half)
        ]
        firsts.append(first)
        downs.append(down_lanes(own_labels))
        alongs.append(jnp.where(other_labels < 0, -3, other_labels))
    columns = []
    folds = [None, None]

    def score(start):
        first = firsts[start // half]
        return products(own_ref[pl.ds(first, half), :], other_ref[pl.ds(start, BLOCK), :])

    def reduce(scores, start):
        turn = start // half
        begin = start - turn * half
        kept = matched(scores, downs[turn], alongs[turn][:, begin : begin + BLOCK])
        columns.append(along_lanes(jnp.max(kept, axis=0, keepdims=True)))
        fold = fold_lanes(kept)
        folds[turn] = fold if folds[turn] is None else jnp.maximum(folds[turn], fold)
        if begin + BLOCK == half:
            part = pl.ds(pl.multiple_of((side ^ turn) * tiles, tiles), tiles)
            own_best_ref[part, :] = jnp.maximum(best_ref[part, :], across(folds[turn]))

    pipelined(score, reduce, copies, CROSS_WAITS)
    other_best_ref[...] = jnp.concatenate(columns, axis=0)


def vmem():
    return pl.BlockSpec(memory_space=pltpu.VMEM)


def smem():
    return pl.BlockSpec(memory_space=pltpu.SMEM)


def anywhere():
    return pl.BlockSpec(memory_space=pl.ANY)


def per_device(embeddings, send_row, slot_cluster):
    rows, width = embeddings.shape
    tiles = width // LANES
    groups = rows // SUBLANES
    side = lax.axis_index("grp").astype(jnp.int32).reshape(1)
    labels = slot_cluster.reshape(1, -1)
    row_shape = jax.ShapeDtypeStruct((rows, width), jnp.bfloat16)
    best_shape = jax.ShapeDtypeStruct((rows // LANES, LANES), jnp.float32)

    unit = pl.pallas_call(
        unit_rows_kernel,
        out_shape=pltpu.VMEM((rows, width), jnp.bfloat16),
        in_specs=[anywhere(), anywhere()],
        out_specs=vmem(),
        scratch_shapes=[
            pltpu.VMEM((rows, width), jnp.bfloat16),
            pltpu.VMEM(((groups + 1) * (tiles + 1) * STRIDE, LANES), jnp.float32),
            pltpu.VMEM(((groups + 1) * tiles * STRIDE, LANES), jnp.float32),
            pltpu.VMEM((rows, LANES), jnp.float32),
            pltpu.VMEM((1, rows), jnp.int32),
            pltpu.VMEM((1, rows), jnp.int32),
            pltpu.SMEM((1, rows), jnp.int32),
            pltpu.SemaphoreType.DMA,
            pltpu.SemaphoreType.DMA,
            pltpu.SemaphoreType.DMA((PARTS,)),
        ],
        compiler_params=pltpu.CompilerParams(vmem_limit_bytes=59 << 20),
        cost_estimate=pl.CostEstimate(
            flops=8 * rows * width, bytes_accessed=4 * rows * width, transcendentals=rows
        ),
        name="unit_rows",
    )(send_row, embeddings)

    own = lax.all_to_all(unit, ("shard", "grp"), split_axis=0, concat_axis=0, tiled=True)
    other = lax.ppermute(own, "grp", [(0, 1), (1, 0)])

    own_best, own_kept = pl.pallas_call(
        own_pairs_kernel,
        out_shape=[best_shape, row_shape],
        in_specs=[smem(), vmem(), anywhere()],
        out_specs=[vmem(), vmem()],
        scratch_shapes=[
            pltpu.VMEM((rows, LANES), jnp.float32),
            pltpu.SemaphoreType.DMA((rows // BLOCK,)),
        ],
        compiler_params=pltpu.CompilerParams(vmem_limit_bytes=26 << 20),
        cost_estimate=pl.CostEstimate(
            flops=rows * rows * width, bytes_accessed=2 * rows * width, transcendentals=0
        ),
        name="own_pairs",
    )(side, labels, own)

    own_best, other_best = pl.pallas_call(
        cross_pairs_kernel,
        out_shape=[best_shape, best_shape],
        in_specs=[smem(), vmem(), vmem(), vmem(), anywhere()],
        out_specs=[vmem(), vmem()],
        scratch_shapes=[
            pltpu.VMEM((rows, width), jnp.bfloat16),
            pltpu.SemaphoreType.DMA((rows // BLOCK,)),
        ],
        compiler_params=pltpu.CompilerParams(vmem_limit_bytes=26 << 20),
        cost_estimate=pl.CostEstimate(
            flops=rows * rows * width, bytes_accessed=4 * rows * width, transcendentals=0
        ),
        name="cross_pairs",
    )(side, labels, own_best, own_kept, other)

    returned = lax.ppermute(other_best, "grp", [(0, 1), (1, 0)])
    return jnp.maximum(own_best, returned).reshape(rows)


def solution(mesh):
    placed = (P(("shard", "grp"), None), P(("shard", "grp"), None), P("shard"))
    return jax.shard_map(
        per_device, mesh=mesh, in_specs=placed, out_specs=P(("shard", "grp")), check_vma=False
    )
```

```python
import jax
import jax.numpy as jnp
from jax import lax
from jax.experimental import pallas as pl
from jax.experimental.pallas import tpu as pltpu
from jax.sharding import PartitionSpec as P

LANES = 128
SUBLANES = 8
STRIDE = SUBLANES + 1
BLOCK = 256
PARTS = 4
OWN_WAITS = {0: 2, 2: 8}
CROSS_WAITS = {0: 2, 2: 8}
UNROLL = 128
ROWS_BY_ROWS = (((1,), (1,)), ((), ()))


def down_lanes(row):
    parts = [
        jnp.transpose(jnp.broadcast_to(row[:, j : j + LANES], (LANES, LANES)))
        for j in range(0, row.shape[1], LANES)
    ]
    return jnp.concatenate(parts, axis=0)


def fold_lanes(values):
    best = values[:, :LANES]
    for j in range(LANES, values.shape[1], LANES):
        best = jnp.maximum(best, values[:, j : j + LANES])
    return best


def across(values):
    parts = [
        jnp.max(jnp.transpose(values[i : i + LANES]), axis=0, keepdims=True)
        for i in range(0, values.shape[0], LANES)
    ]
    return jnp.concatenate(parts, axis=0)


def along_lanes(row):
    return jnp.concatenate([row[:, j : j + LANES] for j in range(0, row.shape[1], LANES)], axis=0)


def add_lanes(values):
    terms = []
    for _ in range(3):
        term = values.astype(jnp.bfloat16)
        terms.append(term)
        values = values - term.astype(jnp.float32)
    ones = jnp.ones((3 * LANES, LANES), jnp.bfloat16)
    return jnp.dot(jnp.concatenate(terms, axis=1), ones, preferred_element_type=jnp.float32)


def unit_rows_kernel(
    index_ref,
    rows_ref,
    unit_ref,
    rows_buf,
    source,
    target,
    squares,
    index_buf,
    place_buf,
    place_smem,
    index_sem,
    place_sem,
    in_sem,
):
    rows, width = rows_ref.shape
    tiles = width // LANES
    group_in = (tiles + 1) * STRIDE
    group_out = tiles * STRIDE
    part = rows // PARTS

    def copy_in(p):
        span = pl.ds(p * part, part)
        return pltpu.make_async_copy(rows_ref.at[span, :], rows_buf.at[span, :], in_sem.at[p])

    copy_index = pltpu.make_async_copy(index_ref, index_buf, index_sem)
    copy_index.start()
    for p in range(PARTS):
        copy_in(p).start()
    empty = rows // SUBLANES * group_in
    source[pl.ds(empty, group_in), :] = jnp.zeros((group_in, LANES), jnp.float32)
    copy_place = pltpu.make_async_copy(place_buf, place_smem, place_sem)

    for p in range(PARTS):
        copy_in(p).wait()

        @pl.loop(0, part // UNROLL)
        def _(c):
            first = pl.multiple_of(p * part + c * UNROLL, UNROLL)
            held = rows_buf[pl.ds(first, UNROLL), :].astype(jnp.float32)
            total = jnp.zeros((UNROLL, LANES), jnp.float32)
            for j in range(tiles):
                piece = held[:, j * LANES : (j + 1) * LANES]
                total = total + piece * piece
                for i in range(UNROLL // SUBLANES):
                    start = (first // SUBLANES + i) * group_in + j * STRIDE
                    source[pl.ds(start, SUBLANES), :] = piece[i * SUBLANES : (i + 1) * SUBLANES]
            squares[pl.ds(first, UNROLL), :] = total

        if p == 0:
            copy_index.wait()
            index = index_buf[...]
            place_buf[...] = jnp.where(
                index < 0, empty, index + (index >> 3) * (group_in - SUBLANES)
            )
            copy_place.start()

    scale = lax.rsqrt(add_lanes(squares[...]) + 1e-06)
    for i in range(rows // SUBLANES):
        start = i * group_in + tiles * STRIDE
        source[pl.ds(start, SUBLANES), :] = scale[i * SUBLANES : (i + 1) * SUBLANES]
    copy_place.wait()

    def move(first):
        base = first // SUBLANES * group_out
        for s in range(UNROLL):
            place = place_smem[0, first + s]
            row = source[pl.ds(place, tiles, stride=STRIDE), :]
            factor = source[pl.ds(place + tiles * STRIDE, 1), :]
            start = base + s // SUBLANES * group_out + s % SUBLANES
            target[pl.ds(start, tiles, stride=STRIDE), :] = row * factor

    def write(first):
        base = first // SUBLANES * group_out
        groups = []
        for i in range(UNROLL // SUBLANES):
            start = base + i * group_out
            pieces = [target[pl.ds(start + j * STRIDE, SUBLANES), :] for j in range(tiles)]
            groups.append(jnp.concatenate(pieces, axis=1))
        unit_ref[pl.ds(pl.multiple_of(first, UNROLL), UNROLL), :] = jnp.concatenate(
            groups, axis=0
        ).astype(jnp.bfloat16)

    move(0)

    @pl.loop(1, rows // UNROLL)
    def _(c):
        write((c - 1) * UNROLL)
        move(c * UNROLL)

    write(rows - UNROLL)


def products(left, right):
    return lax.dot_general(left, right, ROWS_BY_ROWS, preferred_element_type=jnp.float32)


def matched(scores, down, along):
    keep = [down == along[:, j : j + LANES] for j in range(0, along.shape[1], LANES)]
    return jnp.where(jnp.concatenate(keep, axis=1), scores, -1.0)


def copies_in(source, target, sem):
    rows = target.shape[0]
    copies = [
        pltpu.make_async_copy(
            source.at[pl.ds(start, BLOCK), :], target.at[pl.ds(start, BLOCK), :], sem.at[i]
        )
        for i, start in enumerate(range(0, rows, BLOCK))
    ]
    for copy in copies:
        copy.start()
    return copies


def pipelined(score, reduce, copies, waits):
    scores = None
    for i in range(len(copies)):
        if i in waits:
            for copy in copies[i : waits[i]]:
                copy.wait()
        ahead = score(i * BLOCK)
        if scores is not None:
            reduce(scores, (i - 1) * BLOCK)
        scores = ahead
    reduce(scores, (len(copies) - 1) * BLOCK)


def own_pairs_kernel(side_ref, labels_ref, own_hbm, best_ref, own_ref, fold_ref, sem):
    rows = own_ref.shape[0]
    copies = copies_in(own_hbm, own_ref, sem)
    labels = labels_ref[:, pl.ds(pl.multiple_of(side_ref[0] * rows, rows), rows)]
    down = down_lanes(labels)
    along = jnp.where(labels < 0, -3, labels)
    fold_ref[...] = jnp.full(fold_ref.shape, -1.0, jnp.float32)
    columns = []

    def score(start):
        return products(own_ref[pl.ds(0, start + BLOCK), :], own_ref[pl.ds(start, BLOCK), :])

    def reduce(scores, start):
        height = start + BLOCK
        kept = matched(scores, down[:height], along[:, start : start + BLOCK])
        row_id = lax.broadcasted_iota(jnp.int32, (BLOCK, BLOCK), 0)
        column_id = lax.broadcasted_iota(jnp.int32, (BLOCK, BLOCK), 1)
        square = jnp.where(row_id != column_id, kept[start:], -1.0)
        kept = jnp.concatenate([kept[:start], square], axis=0) if start else square
        columns.append(along_lanes(jnp.max(kept, axis=0, keepdims=True)))
        part = pl.ds(0, height)
        fold_ref[part, :] = jnp.maximum(fold_ref[part, :], fold_lanes(kept))

    pipelined(score, reduce, copies, OWN_WAITS)
    best_ref[...] = jnp.maximum(jnp.concatenate(columns, axis=0), across(fold_ref[...]))


def cross_pairs_kernel(
    side_ref, labels_ref, best_ref, own_ref, other_hbm, own_best_ref, other_best_ref, other_ref, sem
):
    rows = own_ref.shape[0]
    half = rows // 2
    tiles = half // LANES
    side = side_ref[0]
    copies = copies_in(other_hbm, other_ref, sem)
    firsts, downs, alongs = [], [], []
    for turn in range(2):
        first = pl.multiple_of((side ^ turn) * half, half)
        own_labels = labels_ref[:, pl.ds(pl.multiple_of(side * rows + first, half), half)]
        other_labels = labels_ref[
            :, pl.ds(pl.multiple_of((1 - side) * rows + turn * half, half), half)
        ]
        firsts.append(first)
        downs.append(down_lanes(own_labels))
        alongs.append(jnp.where(other_labels < 0, -3, other_labels))
    columns = []
    folds = [None, None]

    def score(start):
        first = firsts[start // half]
        return products(own_ref[pl.ds(first, half), :], other_ref[pl.ds(start, BLOCK), :])

    def reduce(scores, start):
        turn = start // half
        begin = start - turn * half
        kept = matched(scores, downs[turn], alongs[turn][:, begin : begin + BLOCK])
        columns.append(along_lanes(jnp.max(kept, axis=0, keepdims=True)))
        fold = fold_lanes(kept)
        folds[turn] = fold if folds[turn] is None else jnp.maximum(folds[turn], fold)
        if begin + BLOCK == half:
            part = pl.ds(pl.multiple_of((side ^ turn) * tiles, tiles), tiles)
            own_best_ref[part, :] = jnp.maximum(best_ref[part, :], across(folds[turn]))

    pipelined(score, reduce, copies, CROSS_WAITS)
    other_best_ref[...] = jnp.concatenate(columns, axis=0)


def vmem():
    return pl.BlockSpec(memory_space=pltpu.VMEM)


def smem():
    return pl.BlockSpec(memory_space=pltpu.SMEM)


def anywhere():
    return pl.BlockSpec(memory_space=pl.ANY)


def per_device(embeddings, send_row, slot_cluster):
    rows, width = embeddings.shape
    tiles = width // LANES
    groups = rows // SUBLANES
    side = lax.axis_index("grp").astype(jnp.int32).reshape(1)
    labels = slot_cluster.reshape(1, -1)
    row_shape = jax.ShapeDtypeStruct((rows, width), jnp.bfloat16)
    best_shape = jax.ShapeDtypeStruct((rows // LANES, LANES), jnp.float32)

    unit = pl.pallas_call(
        unit_rows_kernel,
        out_shape=pltpu.VMEM((rows, width), jnp.bfloat16),
        in_specs=[anywhere(), anywhere()],
        out_specs=vmem(),
        scratch_shapes=[
            pltpu.VMEM((rows, width), jnp.bfloat16),
            pltpu.VMEM(((groups + 1) * (tiles + 1) * STRIDE, LANES), jnp.float32),
            pltpu.VMEM(((groups + 1) * tiles * STRIDE, LANES), jnp.float32),
            pltpu.VMEM((rows, LANES), jnp.float32),
            pltpu.VMEM((1, rows), jnp.int32),
            pltpu.VMEM((1, rows), jnp.int32),
            pltpu.SMEM((1, rows), jnp.int32),
            pltpu.SemaphoreType.DMA,
            pltpu.SemaphoreType.DMA,
            pltpu.SemaphoreType.DMA((PARTS,)),
        ],
        compiler_params=pltpu.CompilerParams(vmem_limit_bytes=59 << 20),
        cost_estimate=pl.CostEstimate(
            flops=8 * rows * width, bytes_accessed=4 * rows * width, transcendentals=rows
        ),
        name="unit_rows",
    )(send_row, embeddings)

    own = lax.all_to_all(unit, ("shard", "grp"), split_axis=0, concat_axis=0, tiled=True)
    other = lax.ppermute(own, "grp", [(0, 1), (1, 0)])

    own_best, own_kept = pl.pallas_call(
        own_pairs_kernel,
        out_shape=[best_shape, row_shape],
        in_specs=[smem(), vmem(), anywhere()],
        out_specs=[vmem(), vmem()],
        scratch_shapes=[
            pltpu.VMEM((rows, LANES), jnp.float32),
            pltpu.SemaphoreType.DMA((rows // BLOCK,)),
        ],
        compiler_params=pltpu.CompilerParams(vmem_limit_bytes=26 << 20),
        cost_estimate=pl.CostEstimate(
            flops=rows * rows * width, bytes_accessed=2 * rows * width, transcendentals=0
        ),
        name="own_pairs",
    )(side, labels, own)

    own_best, other_best = pl.pallas_call(
        cross_pairs_kernel,
        out_shape=[best_shape, best_shape],
        in_specs=[smem(), vmem(), vmem(), vmem(), anywhere()],
        out_specs=[vmem(), vmem()],
        scratch_shapes=[
            pltpu.VMEM((rows, width), jnp.bfloat16),
            pltpu.SemaphoreType.DMA((rows // BLOCK,)),
        ],
        compiler_params=pltpu.CompilerParams(vmem_limit_bytes=26 << 20),
        cost_estimate=pl.CostEstimate(
            flops=rows * rows * width, bytes_accessed=4 * rows * width, transcendentals=0
        ),
        name="cross_pairs",
    )(side, labels, own_best, own_kept, other)

    returned = lax.ppermute(other_best, "grp", [(0, 1), (1, 0)])
    return jnp.maximum(own_best, returned).reshape(rows)


def solution(mesh):
    placed = (P(("shard", "grp"), None), P(("shard", "grp"), None), P("shard"))
    return jax.shard_map(
        per_device, mesh=mesh, in_specs=placed, out_specs=P(("shard", "grp")), check_vma=False
    )
```
